32 devices in a mesh: clique: 2 (over core), dp: 4 (over z), hst: 4 (over y, x).
Axes of the slice: x: 2, y: 2, z: 4, core: 2. Of those that a mesh axis runs over, the one named last changes fastest.
Arguments:
- hot_table: bfloat16 [4096, 1024], P('clique'), may hold values from -6 to 6
- cold_table: bfloat16 [8192, 1024], P('hst'), may hold values from -6 to 6
- seed_source: int32 [32, 64], P(('clique', 'dp', 'hst')), may hold values from 0 to 5119, as said below
- hop1_source: int32 [32, 640], P(('clique', 'dp', 'hst')), may hold values from 0 to 5119, as said below
- hop2_source: int32 [32, 9600], P(('clique', 'dp', 'hst')), may hold values from 0 to 5119, as said below
- cold_ask: int32 [32, 4, 256], P(('clique', 'dp', 'hst')), may hold values from 0 to 2047, as said below
- cotangent: bfloat16 [2048, 1024], P(('clique', 'dp', 'hst')), may hold values from -0.13183594 to 0.13183594
- w1_self: bfloat16 [1024, 1024], replicated, may hold values from -0.1875 to 0.1875
- w1_neigh: bfloat16 [1024, 1024], replicated, may hold values from -0.1875 to 0.1875
- w2_self: bfloat16 [1024, 1024], replicated, may hold values from -0.1875 to 0.1875
- w2_neigh: bfloat16 [1024, 1024], replicated, may hold values from -0.1875 to 0.1875
Outputs:
- embedding: bfloat16 [2048, 1024], P(('clique', 'dp', 'hst'))
- grad_w1_self: float32 [1024, 1024], P(('clique', 'hst'))
- grad_w1_neigh: float32 [1024, 1024], P(('clique', 'hst'))
- grad_w2_self: float32 [1024, 1024], P(('clique', 'hst'))
- grad_w2_neigh: float32 [1024, 1024], P(('clique', 'hst'))
The draws below stay inside these ranges and needn't reach their ends.
Inputs may be any that keep to these rules, and one draw needn't show every extreme that they name: `seed_source`: values below 4096 name a hot cache row; a value 4096 + o * 256 + s names slot s of this device's request to cold owner o. Every slot of every owner is named by at least one node of the device's tree (seed, first-hop or second-hop). `hop1_source`: as for seed_source. `hop2_source`: as for seed_source. `cold_ask`: each entry is a row within the owner's block of cold_table.
All inputs are finite; a program needn't handle non-finite values.
Results may differ from the reference program's by a relative error of at most 0.0044.
The reference program's roundings to bfloat16 on the way (of `level_mean`, `hidden`, `hidden_mean` and `grad_pre`) count: a program that leaves them out, or rounds other values in their place, can miss the bound.
Values may be sent and summed in bfloat16 or wider, within the bound.
A program may use at most 128 MiB of HBM per device.

```python
import jax
import jax.numpy as jnp
from jax import lax

F = 1024
H = 1024
K2 = 10
K1 = 15
SEEDS = 64
HOT = 4096
COLD_DEV = 2048
CAP = 256
OWNERS = 4
WORKERS = 32
ALL_SEEDS = 2048
HOP1 = 640
COLD_ROWS = 8192


def sampled_tree(key):
    key = jax.random.fold_in(key, 7301)
    subkeys = jax.random.split(key, 8)
    requests = jax.random.randint(subkeys[3], (WORKERS, OWNERS, CAP), 0, COLD_DEV)
    node_total = SEEDS * (1 + K2 + K2 * K1)
    slots_total = OWNERS * CAP
    ranks = jnp.arange(node_total)[None, :]
    spare_cold = HOT + jax.random.randint(subkeys[4], (WORKERS, node_total), 0, slots_total)
    hot_source = jax.random.randint(subkeys[5], (WORKERS, node_total), 0, HOT)
    picker = jax.random.randint(subkeys[6], (WORKERS, node_total), 0, 2)
    by_rank = jnp.where(picker == 1, spare_cold, hot_source)
    by_rank = jnp.where(ranks < slots_total, HOT + jnp.minimum(ranks, slots_total - 1), by_rank)
    worker_keys = jax.random.split(subkeys[7], WORKERS)
    orders = jax.vmap(lambda k: jax.random.permutation(k, node_total))(worker_keys)
    source = jnp.take_along_axis(by_rank, orders, axis=1).astype(jnp.int32)
    return (requests.astype(jnp.int32), source)


def draw_seed_source(key, part):
    requests, source = sampled_tree(key)
    return source[:, :SEEDS]


def draw_hop1_source(key, part):
    requests, source = sampled_tree(key)
    return source[:, SEEDS:SEEDS + HOP1]


def draw_hop2_source(key, part):
    requests, source = sampled_tree(key)
    return source[:, SEEDS + HOP1:]


def draw_cold_ask(key, part):
    requests, source = sampled_tree(key)
    return requests


def level_of(rng, extent, pieces, low, largest):
    level, own = 1.0, jax.random.fold_in(rng, 6)
    for dim, shards_of in pieces:
        draws = jnp.exp(jax.random.uniform(jax.random.fold_in(own, dim), (shards_of,), jnp.float32, low / len(pieces), largest / len(pieces)))
        level = level * jnp.repeat(draws, extent[dim] // shards_of).reshape([-1 if axis == dim else 1 for axis in range(len(extent))])
    return level


def bell_draw(stream_key, dims, deviation, bound, cuts=(), held_as=jnp.bfloat16):
    array = jax.random.normal(stream_key, dims, jnp.float32) * deviation
    if len(cuts) > 0:
        array = level_of(stream_key, dims, cuts, -0.22, 0.18) * array
    return jnp.clip(array, min=-bound, max=bound).astype(held_as)


def setup_inputs(seed: int = 0) -> dict:
    arg_keys = jax.random.split(jax.random.key(seed), 12)
    hot_table = bell_draw(arg_keys[0], (HOT, F), 1.0, 6.0, ((0, 2),))
    cold_table = bell_draw(arg_keys[1], (COLD_ROWS, F), 1.0, 6.0, ((0, 4),))
    seed_source = draw_seed_source(jax.random.fold_in(arg_keys[11], 71), 0)
    hop1_source = draw_hop1_source(jax.random.fold_in(arg_keys[11], 71), 0)
    hop2_source = draw_hop2_source(jax.random.fold_in(arg_keys[11], 71), 0)
    cold_ask = draw_cold_ask(jax.random.fold_in(arg_keys[11], 71), 0)
    cotangent = bell_draw(arg_keys[6], (ALL_SEEDS, H), (ALL_SEEDS ** -0.5), 0.13183594, ((0, 32),))
    w1_self = bell_draw(arg_keys[7], (F, H), F ** -0.5, 0.1875)
    w1_neigh = bell_draw(arg_keys[8], (F, H), F ** -0.5, 0.1875)
    w2_self = bell_draw(arg_keys[9], (H, H), H ** -0.5, 0.1875)
    w2_neigh = bell_draw(arg_keys[10], (H, H), H ** -0.5, 0.1875)
    return {"hot_table": hot_table, "cold_table": cold_table, "seed_source": seed_source, "hop1_source": hop1_source, "hop2_source": hop2_source, "cold_ask": cold_ask, "cotangent": cotangent, "w1_self": w1_self, "w1_neigh": w1_neigh, "w2_self": w2_self, "w2_neigh": w2_neigh}


def fetch(source, hot_table, cold_table, requests):
    is_hot = source < HOT
    hot_pick = jnp.take(hot_table, jnp.clip(source, 0, HOT - 1).astype(jnp.int32), axis=0)
    offset = jnp.clip(source - HOT, 0, OWNERS * CAP - 1).astype(jnp.int32)
    owner = offset // CAP
    slot_index = offset % CAP
    row_index = (requests[owner, slot_index] + owner * COLD_DEV).astype(jnp.int32)
    cold_pick = jnp.take(cold_table, row_index, axis=0)
    return jnp.where(is_hot[:, None], hot_pick, cold_pick)


def mean_rows(values, fanout):
    groups = values.shape[0] // fanout
    total = jnp.sum(values.reshape(groups, fanout, values.shape[1]), axis=1, dtype=jnp.float32)
    return (total / fanout).astype(jnp.bfloat16)


def matmul(left, right):
    return jnp.dot(left, right, preferred_element_type=jnp.float32)


def inner_rows(left, right):
    return lax.dot_general(left, right, (((0,), (0,)), ((), ())), preferred_element_type=jnp.float32)


def inner_cols(left, right):
    return lax.dot_general(left, right, (((1,), (1,)), ((), ())), preferred_element_type=jnp.float32)


def reference(hot_table, cold_table, seed_source, hop1_source, hop2_source, cold_ask, cotangent, w1_self, w1_neigh, w2_self, w2_neigh):
    cot_blocks = cotangent.reshape(WORKERS, SEEDS, H)

    def one_worker(totals, items):
        seeds_src, first_src, second_src, requests, cot = items
        seed_feat = fetch(seeds_src, hot_table, cold_table, requests)
        hop1_feat = fetch(first_src, hot_table, cold_table, requests)
        hop2_feat = fetch(second_src, hot_table, cold_table, requests)
        level_in = jnp.concatenate([seed_feat, hop1_feat], 0)
        level_mean = jnp.concatenate([mean_rows(hop1_feat, K2), mean_rows(hop2_feat, K1)], 0)
        pre = matmul(level_in, w1_self) + matmul(level_mean, w1_neigh)
        hidden = jnp.maximum(pre, 0.0).astype(jnp.bfloat16)
        hidden_seed = hidden[:SEEDS]
        hidden_mean = mean_rows(hidden[SEEDS:], K2)
        embed = (matmul(hidden_seed, w2_self) + matmul(hidden_mean, w2_neigh)).astype(jnp.bfloat16)
        grad_seed = inner_cols(cot, w2_self)
        grad_mean = inner_cols(cot, w2_neigh) / K2
        grad_hop = jnp.broadcast_to(grad_mean[:, None, :], (SEEDS, K2, H)).reshape(SEEDS * K2, H)
        grad_hidden = jnp.concatenate([grad_seed, grad_hop], 0)
        grad_pre = jnp.where(pre > 0, grad_hidden, jnp.float32(0.0)).astype(jnp.bfloat16)
        terms = (inner_rows(level_in, grad_pre), inner_rows(level_mean, grad_pre),
                 inner_rows(hidden_seed, cot), inner_rows(hidden_mean, cot))
        return tuple(a + b for a, b in zip(totals, terms)), embed

    start = (jnp.zeros((F, H), jnp.float32), jnp.zeros((F, H), jnp.float32),
             jnp.zeros((H, H), jnp.float32), jnp.zeros((H, H), jnp.float32))
    totals, embeds = lax.scan(one_worker, start, (seed_source, hop1_source, hop2_source, cold_ask, cot_blocks))
    embedding = embeds.reshape(ALL_SEEDS, H)
    return (embedding, totals[0], totals[1], totals[2], totals[3])
```

```python
import jax
import jax.numpy as jnp
from jax import lax
from jax.experimental import pallas as pl
from jax.experimental.pallas import tpu as pltpu
from jax.sharding import PartitionSpec as P

LANES = 128
F32 = jnp.float32
BF16 = jnp.bfloat16


def inner_rows(left, right):
    return lax.dot_general(left, right, (((0,), (0,)), ((), ())), preferred_element_type=F32)


def inner_cols(left, right):
    return lax.dot_general(left, right, (((1,), (1,)), ((), ())), preferred_element_type=F32)


def matmul(left, right):
    return jnp.dot(left, right, preferred_element_type=F32)


def tree_sum(items):
    while len(items) > 1:
        rest = items[2 * (len(items) // 2):]
        items = [items[i] + items[i + 1] for i in range(0, len(items) - 1, 2)] + rest
    return items[0]


def mean_rows(values, fanout):
    groups = values.shape[0] // fanout
    total = jnp.sum(values.reshape(groups, fanout, values.shape[1]), axis=1, dtype=F32)
    return (total / fanout).astype(BF16)


def pick_kernel(ask_ref, table_ref, out_ref):
    count = ask_ref.shape[0]
    step = 16

    def some(i, carry):
        for j in range(step):
            out_ref[i * step + j] = table_ref[ask_ref[i * step + j]]
        return carry

    lax.fori_loop(0, count // step, some, 0)


def pick_rows(ask, table):
    count, tile = ask.shape[0], table.shape[1:]
    nbytes = (table.shape[0] + count) * tile[0] * tile[1] * 2
    return pl.pallas_call(
        pick_kernel,
        out_shape=jax.ShapeDtypeStruct((count,) + tile, table.dtype),
        in_specs=[
            pl.BlockSpec(memory_space=pltpu.SMEM),
            pl.BlockSpec(memory_space=pltpu.VMEM),
        ],
        out_specs=pl.BlockSpec(memory_space=pltpu.VMEM),
        compiler_params=pltpu.CompilerParams(vmem_limit_bytes=nbytes + (8 << 20)),
        cost_estimate=pl.CostEstimate(flops=0, bytes_accessed=4 * nbytes, transcendentals=0),
        name="pick_rows",
    )(ask, table)


def tree_kernel(seed_ref, hop1_ref, hop2_ref, hot_ref, cold_ref, in_ref, mean_ref, table, sems):
    hot_rows = hot_ref.shape[0]
    seeds, hop1, hop2 = seed_ref.shape[0], hop1_ref.shape[0], hop2_ref.shape[0]
    k2, k1 = hop1 // seeds, hop2 // hop1
    loads = (
        pltpu.make_async_copy(hot_ref, table.at[pl.ds(0, hot_rows)], sems.at[0]),
        pltpu.make_async_copy(cold_ref, table.at[pl.ds(hot_rows, cold_ref.shape[0])], sems.at[1]),
    )
    for load in loads:
        load.start()
    for load in loads:
        load.wait()

    def one_seed(s, carry):
        in_ref[s] = table[seed_ref[s]]
        rows = []
        for j in range(k2):
            row = table[hop1_ref[s * k2 + j]]
            in_ref[seeds + s * k2 + j] = row
            rows.append(row.astype(F32))
        mean_ref[s] = (tree_sum(rows) / k2).astype(BF16)
        return carry

    lax.fori_loop(0, seeds, one_seed, 0)

    def one_node(n, carry):
        for u in range(2):
            m = n * 2 + u
            rows = [table[hop2_ref[m * k1 + j]].astype(F32) for j in range(k1)]
            mean_ref[seeds + m] = (tree_sum(rows) / k1).astype(BF16)
        return carry

    lax.fori_loop(0, hop1 // 2, one_node, 0)


def gather_tree(seed, hop1, hop2, hot, cold):
    tile = hot.shape[1:]
    nodes = seed.shape[0] + hop1.shape[0]
    table_rows = hot.shape[0] + cold.shape[0]
    row_bytes = tile[0] * tile[1] * 2
    out = jax.ShapeDtypeStruct((nodes,) + tile, BF16)
    return pl.pallas_call(
        tree_kernel,
        out_shape=(out, out),
        in_specs=[pl.BlockSpec(memory_space=pltpu.SMEM)] * 3 + [pl.BlockSpec(memory_space=pl.ANY)] * 2,
        out_specs=(pl.BlockSpec(memory_space=pltpu.VMEM),) * 2,
        scratch_shapes=[
            pltpu.VMEM((table_rows,) + tile, BF16),
            pltpu.SemaphoreType.DMA((2,)),
        ],
        compiler_params=pltpu.CompilerParams(
            vmem_limit_bytes=(table_rows + 2 * nodes) * row_bytes + (8 << 20)
        ),
        cost_estimate=pl.CostEstimate(
            flops=0, bytes_accessed=8 * table_rows * row_bytes, transcendentals=0
        ),
        name="gather_tree",
    )(seed, hop1, hop2, hot, cold)


def body(
    hot_table,
    cold_table,
    seed_source,
    hop1_source,
    hop2_source,
    cold_ask,
    cotangent,
    w1_self,
    w1_neigh,
    w2_self,
    w2_neigh,
):
    width = hot_table.shape[1]
    hidden_width = w1_self.shape[1]
    seeds = seed_source.shape[1]
    hop1 = hop1_source.shape[1]
    k2 = hop1 // seeds
    owners, cap = cold_ask.shape[1], cold_ask.shape[2]
    cliques = lax.axis_size("clique")
    hosts = lax.axis_size("hst")
    planes = lax.axis_size("dp")
    tile = (width // LANES, LANES)

    asked = lax.all_to_all(cold_ask[0], "hst", split_axis=0, concat_axis=0, tiled=True)
    hot_tiles = hot_table.reshape((hot_table.shape[0],) + tile)
    hot_full = lax.all_gather(hot_tiles, "clique", axis=0, tiled=True)
    cold_tiles = cold_table.reshape((cold_table.shape[0],) + tile)
    picked = pick_rows(asked.reshape(-1), cold_tiles).reshape((owners, cap) + tile)
    cold_rows = lax.all_to_all(picked, "hst", split_axis=0, concat_axis=0, tiled=True)
    cot_all = lax.all_gather(cotangent, ("clique", "dp", "hst"), axis=0, tiled=True)

    grad_seed = inner_cols(cotangent, w2_self)
    grad_mean = inner_cols(cotangent, w2_neigh) / k2

    in_tiles, mean_tiles = gather_tree(
        seed_source[0], hop1_source[0], hop2_source[0], hot_full, cold_rows.reshape((-1,) + tile)
    )
    level_in = in_tiles.reshape(-1, width)
    level_mean = mean_tiles.reshape(-1, width)

    pre = matmul(level_in, w1_self) + matmul(level_mean, w1_neigh)
    hidden = jnp.maximum(pre, 0.0).astype(BF16)
    hidden_seed = hidden[:seeds]
    hidden_mean = mean_rows(hidden[seeds:], k2)
    embedding = (matmul(hidden_seed, w2_self) + matmul(hidden_mean, w2_neigh)).astype(BF16)

    grad_hop = jnp.broadcast_to(grad_mean[:, None, :], (seeds, k2, hidden_width)).reshape(
        seeds * k2, hidden_width
    )
    grad_hidden = jnp.concatenate([grad_seed, grad_hop], 0)
    grad_pre = jnp.where(pre > 0, grad_hidden, 0.0).astype(BF16)

    me = lax.axis_index("clique")
    half = width // cliques
    share = half // hosts

    def terms(c):
        return [
            inner_rows(lax.dynamic_slice_in_dim(level, c * half, half, 1), grad_pre)
            for level in (level_in, level_mean)
        ]

    total = terms(me)
    for k in range(1, cliques):
        away = [t.astype(BF16) for t in terms(lax.rem(me + k, cliques))]
        pairs = [(c, (c + k) % cliques) for c in range(cliques)]
        got = [lax.ppermute(t, "clique", pairs) for t in away]
        total = [t + g.astype(F32) for t, g in zip(total, got)]
    stacked = jnp.stack([t.astype(BF16).reshape(hosts, share, hidden_width) for t in total], 1)
    parts = lax.all_to_all(stacked, "hst", split_axis=0, concat_axis=0, tiled=True)
    shares = jnp.sum(parts, axis=0, dtype=F32).astype(BF16)
    slabs = lax.all_gather(shares, "dp", axis=0)
    grad_w1 = jnp.sum(slabs, axis=0, dtype=F32)

    shares2 = cliques * hosts
    both = jnp.stack([hidden_seed, hidden_mean], 1).reshape(seeds, 2, shares2, -1)
    both = lax.all_to_all(
        both.transpose(2, 0, 1, 3).reshape(shares2, seeds, -1),
        ("clique", "hst"), split_axis=0, concat_axis=0, tiled=True,
    )
    both = lax.all_gather(both.reshape(cliques, hosts * seeds, -1), "dp", axis=1)
    grad_w2 = inner_rows(both.reshape(cot_all.shape[0], -1), cot_all)
    cut = grad_w2.shape[0] // 2
    return (embedding, grad_w1[0], grad_w1[1], grad_w2[:cut], grad_w2[cut:])


def solution(mesh):
    workers = P(("clique", "dp", "hst"), None)
    rows = P(("clique", "hst"), None)
    in_specs = (
        P("clique", None), P("hst", None), workers, workers, workers,
        P(("clique", "dp", "hst"), None, None), workers, P(), P(), P(), P(),
    )
    return jax.shard_map(
        body, mesh=mesh, in_specs=in_specs, out_specs=(workers, rows, rows, rows, rows), check_vma=False
    )
```

```python
import jax
import jax.numpy as jnp
from jax import lax
from jax.experimental import pallas as pl
from jax.experimental.pallas import tpu as pltpu
from jax.sharding import PartitionSpec as P

LANES = 128
F32 = jnp.float32
BF16 = jnp.bfloat16


def inner_rows(left, right):
    return lax.dot_general(left, right, (((0,), (0,)), ((), ())), preferred_element_type=F32)


def inner_cols(left, right):
    return lax.dot_general(left, right, (((1,), (1,)), ((), ())), preferred_element_type=F32)


def matmul(left, right):
    return jnp.dot(left, right, preferred_element_type=F32)


def tree_sum(items):
    while len(items) > 1:
        rest = items[2 * (len(items) // 2):]
        items = [items[i] + items[i + 1] for i in range(0, len(items) - 1, 2)] + rest
    return items[0]


def pick_kernel(ask_ref, table_ref, out_ref):
    count = ask_ref.shape[0]
    step = 16

    def some(i, carry):
        for j in range(step):
            out_ref[i * step + j] = table_ref[ask_ref[i * step + j]]
        return carry

    lax.fori_loop(0, count // step, some, 0)


def pick_rows(ask, table):
    count, tile = ask.shape[0], table.shape[1:]
    nbytes = (table.shape[0] + count) * tile[0] * tile[1] * 2
    return pl.pallas_call(
        pick_kernel,
        out_shape=jax.ShapeDtypeStruct((count,) + tile, table.dtype),
        in_specs=[
            pl.BlockSpec(memory_space=pltpu.SMEM),
            pl.BlockSpec(memory_space=pltpu.VMEM),
        ],
        out_specs=pl.BlockSpec(memory_space=pltpu.VMEM),
        compiler_params=pltpu.CompilerParams(vmem_limit_bytes=nbytes + (8 << 20)),
        cost_estimate=pl.CostEstimate(flops=0, bytes_accessed=4 * nbytes, transcendentals=0),
        name="pick_rows",
    )(ask, table)


def tree_kernel(seed_ref, hop1_ref, hop2_ref, hot_ref, cold_ref, in_ref, mean_ref, table, sems):
    hot_rows = hot_ref.shape[0]
    seeds, hop1, hop2 = seed_ref.shape[0], hop1_ref.shape[0], hop2_ref.shape[0]
    k2, k1 = hop1 // seeds, hop2 // hop1
    loads = (
        pltpu.make_async_copy(hot_ref, table.at[pl.ds(0, hot_rows)], sems.at[0]),
        pltpu.make_async_copy(cold_ref, table.at[pl.ds(hot_rows, cold_ref.shape[0])], sems.at[1]),
    )
    for load in loads:
        load.start()
    for load in loads:
        load.wait()

    def one_seed(s, carry):
        in_ref[s] = table[seed_ref[s]]
        rows = []
        for j in range(k2):
            row = table[hop1_ref[s * k2 + j]]
            in_ref[seeds + s * k2 + j] = row
            rows.append(row.astype(F32))
        mean_ref[s] = (tree_sum(rows) / k2).astype(BF16)
        return carry

    lax.fori_loop(0, seeds, one_seed, 0)

    def one_node(n, carry):
        for u in range(2):
            m = n * 2 + u
            rows = [table[hop2_ref[m * k1 + j]].astype(F32) for j in range(k1)]
            mean_ref[seeds + m] = (tree_sum(rows) / k1).astype(BF16)
        return carry

    lax.fori_loop(0, hop1 // 2, one_node, 0)


def gather_tree(seed, hop1, hop2, hot, cold):
    tile = hot.shape[1:]
    nodes = seed.shape[0] + hop1.shape[0]
    table_rows = hot.shape[0] + cold.shape[0]
    row_bytes = tile[0] * tile[1] * 2
    out = jax.ShapeDtypeStruct((nodes,) + tile, BF16)
    return pl.pallas_call(
        tree_kernel,
        out_shape=(out, out),
        in_specs=[pl.BlockSpec(memory_space=pltpu.SMEM)] * 3 + [pl.BlockSpec(memory_space=pl.ANY)] * 2,
        out_specs=(pl.BlockSpec(memory_space=pltpu.VMEM),) * 2,
        scratch_shapes=[
            pltpu.VMEM((table_rows,) + tile, BF16),
            pltpu.SemaphoreType.DMA((2,)),
        ],
        compiler_params=pltpu.CompilerParams(
            vmem_limit_bytes=(table_rows + 2 * nodes) * row_bytes + (8 << 20)
        ),
        cost_estimate=pl.CostEstimate(
            flops=0, bytes_accessed=8 * table_rows * row_bytes, transcendentals=0
        ),
        name="gather_tree",
    )(seed, hop1, hop2, hot, cold)


def reduce_kernel(
    mine0, mine1, away0, away1, out0, out1,
    got1, send2, got2, keep, send3, got3, send4, got4,
    s1, r1, s2, r2, s3, r3, s4, r4,
):
    mine, away, out = (mine0, mine1), (away0, away1), (out0, out1)
    hosts, planes = mine0.shape[0], mine0.shape[1]
    c, d, h = lax.axis_index("clique"), lax.axis_index("dp"), lax.axis_index("hst")
    host = [lax.rem(h + k, hosts) for k in range(hosts)]
    plane = [lax.rem(d + k, planes) for k in range(planes)]
    peers = [{"clique": 1 - c}] + [{"hst": q} for q in host[1:]] + [{"dp": p} for p in plane[1:]]

    barrier = pltpu.get_barrier_semaphore()
    for peer in peers:
        pl.semaphore_signal(barrier, inc=1, device_id=peer, device_id_type=pl.DeviceIdType.MESH)
    pl.semaphore_wait(barrier, len(peers))

    def send(src, dst, sent, landed, peer):
        copy = pltpu.make_async_remote_copy(
            src_ref=src, dst_ref=dst, send_sem=sent, recv_sem=landed,
            device_id=peer, device_id_type=pl.DeviceIdType.MESH,
        )
        copy.start()
        return copy

    first, second, third, fourth = {}, {}, {}, {}
    for m in range(2):
        for k in list(range(1, hosts)) + [0]:
            q = host[k]
            first[m, k] = send(
                away[m].at[q], got1.at[m, q], s1.at[m, k], r1.at[m, k], {"clique": 1 - c}
            )
    for m in range(2):
        for k in range(1, hosts):
            q = host[k]
            first[m, k].wait_recv()
            for p in range(planes):
                send2[m, k - 1, p] = (mine[m][q, p] + got1[m, q, p].astype(F32)).astype(BF16)
            second[m, k] = send(
                send2.at[m, k - 1], got2.at[m, k - 1], s2.at[m, k - 1], r2.at[m, k - 1], {"hst": q}
            )
        first[m, 0].wait_recv()
    for m in range(2):
        for k in range(1, hosts):
            second[m, k].wait_recv()
        for p in range(planes):
            total = mine[m][h, p] + got1[m, h, p].astype(F32)
            for k in range(1, hosts):
                total = total + got2[m, k - 1, p].astype(F32)
            keep[m, p] = total
            send3[m, p] = total.astype(BF16)
        for k in range(1, planes):
            third[m, k] = send(
                send3.at[m, plane[k]], got3.at[m, k - 1], s3.at[m, k - 1], r3.at[m, k - 1],
                {"dp": plane[k]},
            )
    for m in range(2):
        for k in range(1, planes):
            third[m, k].wait_recv()
        total = keep[m, d]
        for k in range(1, planes):
            total = total + got3[m, k - 1].astype(F32)
        send4[m] = total.astype(BF16)
        for k in range(1, planes):
            fourth[m, k] = send(
                send4.at[m], got4.at[m, k - 1], s4.at[m, k - 1], r4.at[m, k - 1], {"dp": plane[k]}
            )
        out[m][d] = send4[m].astype(F32)
    for m in range(2):
        for k in range(1, planes):
            fourth[m, k].wait_recv()
            out[m][lax.rem(d + planes - k, planes)] = got4[m, k - 1].astype(F32)
    for copies in (first, second, third, fourth):
        for copy in copies.values():
            copy.wait_send()


def reduce_pair(mine, away):
    hosts, planes, rows, width = mine[0].shape
    out = jax.ShapeDtypeStruct((planes, rows, width), F32)
    piece = (rows, width)
    return pl.pallas_call(
        reduce_kernel,
        out_shape=(out, out),
        in_specs=[pl.BlockSpec(memory_space=pltpu.VMEM)] * 4,
        out_specs=(pl.BlockSpec(memory_space=pltpu.VMEM),) * 2,
        scratch_shapes=[
            pltpu.VMEM((2, hosts, planes) + piece, BF16),
            pltpu.VMEM((2, hosts - 1, planes) + piece, BF16),
            pltpu.VMEM((2, hosts - 1, planes) + piece, BF16),
            pltpu.VMEM((2, planes) + piece, F32),
            pltpu.VMEM((2, planes) + piece, BF16),
            pltpu.VMEM((2, planes - 1) + piece, BF16),
            pltpu.VMEM((2,) + piece, BF16),
            pltpu.VMEM((2, planes - 1) + piece, BF16),
            pltpu.SemaphoreType.DMA((2, hosts)),
            pltpu.SemaphoreType.DMA((2, hosts)),
        ] + [pltpu.SemaphoreType.DMA((2, hosts - 1))] * 2 + [pltpu.SemaphoreType.DMA((2, planes - 1))] * 4,
        compiler_params=pltpu.CompilerParams(
            collective_id=0, has_side_effects=True, vmem_limit_bytes=40 << 20
        ),
        cost_estimate=pl.CostEstimate(flops=0, bytes_accessed=100 << 20, transcendentals=0),
        name="reduce_pair",
    )(*mine, *away)


def body(
    hot_table,
    cold_table,
    seed_source,
    hop1_source,
    hop2_source,
    cold_ask,
    cotangent,
    w1_self,
    w1_neigh,
    w2_self,
    w2_neigh,
):
    width = hot_table.shape[1]
    hidden_width = w1_self.shape[1]
    seeds = seed_source.shape[1]
    hop1 = hop1_source.shape[1]
    k2 = hop1 // seeds
    owners, cap = cold_ask.shape[1], cold_ask.shape[2]
    cliques = lax.axis_size("clique")
    hosts = lax.axis_size("hst")
    planes = lax.axis_size("dp")
    tile = (width // LANES, LANES)

    asked = lax.all_to_all(cold_ask[0], "hst", split_axis=0, concat_axis=0, tiled=True)
    hot_tiles = hot_table.reshape((hot_table.shape[0],) + tile)
    hot_full = lax.all_gather(hot_tiles, "clique", axis=0, tiled=True)
    cold_tiles = cold_table.reshape((cold_table.shape[0],) + tile)
    picked = pick_rows(asked.reshape(-1), cold_tiles).reshape((owners, cap) + tile)
    cold_rows = lax.all_to_all(picked, "hst", split_axis=0, concat_axis=0, tiled=True)
    cot_all = lax.all_gather(cotangent, ("clique", "dp", "hst"), axis=0, tiled=True)

    grad_seed = inner_cols(cotangent, w2_self)
    grad_mean = inner_cols(cotangent, w2_neigh) / k2

    in_tiles, mean_tiles = gather_tree(
        seed_source[0], hop1_source[0], hop2_source[0], hot_full, cold_rows.reshape((-1,) + tile)
    )
    level_in = in_tiles.reshape(-1, width)
    level_mean = mean_tiles.reshape(-1, width)

    pre = matmul(level_in, w1_self) + matmul(level_mean, w1_neigh)
    hidden = jnp.maximum(pre, 0.0).astype(BF16)
    hidden_seed = hidden[:seeds]
    node = lax.broadcasted_iota(jnp.int32, (seeds, hop1), 1) // k2
    member = (node == lax.broadcasted_iota(jnp.int32, (seeds, hop1), 0)).astype(BF16)
    hidden_mean = (matmul(member, hidden[seeds:]) / k2).astype(BF16)
    embedding = (matmul(hidden_seed, w2_self) + matmul(hidden_mean, w2_neigh)).astype(BF16)

    grad_hop = jnp.broadcast_to(grad_mean[:, None, :], (seeds, k2, hidden_width)).reshape(
        seeds * k2, hidden_width
    )
    grad_hidden = jnp.concatenate([grad_seed, grad_hop], 0)
    grad_pre = jnp.where(pre > 0, grad_hidden, 0.0).astype(BF16)

    shares2 = cliques * hosts
    both = jnp.stack([hidden_seed, hidden_mean], 1).reshape(seeds, 2, shares2, -1)
    both = lax.all_to_all(
        both.transpose(2, 0, 1, 3).reshape(shares2, seeds, -1),
        ("clique", "hst"), split_axis=0, concat_axis=0, tiled=True,
    )
    both = lax.all_gather(both.reshape(cliques, hosts * seeds, -1), "dp", axis=1)
    grad_w2 = inner_rows(both.reshape(cot_all.shape[0], -1), cot_all)

    me = lax.axis_index("clique")
    half = width // cliques
    rows = half // hosts // planes

    def terms(c):
        return [
            inner_rows(lax.dynamic_slice_in_dim(level, c * half, half, 1), grad_pre).reshape(
                hosts, planes, rows, hidden_width
            )
            for level in (level_in, level_mean)
        ]

    away = [t.astype(BF16) for t in terms(1 - me)]
    grad_w1 = [t.reshape(-1, hidden_width) for t in reduce_pair(terms(me), away)]

    cut = grad_w2.shape[0] // 2
    return (embedding, grad_w1[0], grad_w1[1], grad_w2[:cut], grad_w2[cut:])


def solution(mesh):
    workers = P(("clique", "dp", "hst"), None)
    rows = P(("clique", "hst"), None)
    in_specs = (
        P("clique", None), P("hst", None), workers, workers, workers,
        P(("clique", "dp", "hst"), None, None), workers, P(), P(), P(), P(),
    )
    return jax.shard_map(
        body, mesh=mesh, in_specs=in_specs, out_specs=(workers, rows, rows, rows, rows), check_vma=False
    )
```

```python
import jax
import jax.numpy as jnp
from jax import lax
from jax.experimental import pallas as pl
from jax.experimental.pallas import tpu as pltpu
from jax.sharding import PartitionSpec as P

LANES = 128
F32 = jnp.float32
BF16 = jnp.bfloat16


def inner_rows(left, right):
    return lax.dot_general(left, right, (((0,), (0,)), ((), ())), preferred_element_type=F32)


def inner_cols(left, right):
    return lax.dot_general(left, right, (((1,), (1,)), ((), ())), preferred_element_type=F32)


def matmul(left, right):
    return jnp.dot(left, right, preferred_element_type=F32)


def tree_sum(items):
    while len(items) > 1:
        rest = items[2 * (len(items) // 2):]
        items = [items[i] + items[i + 1] for i in range(0, len(items) - 1, 2)] + rest
    return items[0]


def pick_kernel(ask_ref, table_ref, out_ref):
    count = ask_ref.shape[0]
    step = 16

    def some(i, carry):
        for j in range(step):
            out_ref[i * step + j] = table_ref[ask_ref[i * step + j]]
        return carry

    lax.fori_loop(0, count // step, some, 0)


def pick_rows(ask, table):
    count, tile = ask.shape[0], table.shape[1:]
    nbytes = (table.shape[0] + count) * tile[0] * tile[1] * 2
    return pl.pallas_call(
        pick_kernel,
        out_shape=jax.ShapeDtypeStruct((count,) + tile, table.dtype),
        in_specs=[
            pl.BlockSpec(memory_space=pltpu.SMEM),
            pl.BlockSpec(memory_space=pltpu.VMEM),
        ],
        out_specs=pl.BlockSpec(memory_space=pltpu.VMEM),
        compiler_params=pltpu.CompilerParams(vmem_limit_bytes=nbytes + (8 << 20)),
        cost_estimate=pl.CostEstimate(flops=0, bytes_accessed=4 * nbytes, transcendentals=0),
        name="pick_rows",
    )(ask, table)


def tree_kernel(seed_ref, hop1_ref, hop2_ref, hot_ref, cold_ref, in_ref, mean_ref, table, sems):
    hot_rows = hot_ref.shape[0]
    seeds, hop1, hop2 = seed_ref.shape[0], hop1_ref.shape[0], hop2_ref.shape[0]
    k2, k1 = hop1 // seeds, hop2 // hop1
    loads = (
        pltpu.make_async_copy(hot_ref, table.at[pl.ds(0, hot_rows)], sems.at[0]),
        pltpu.make_async_copy(cold_ref, table.at[pl.ds(hot_rows, cold_ref.shape[0])], sems.at[1]),
    )
    for load in loads:
        load.start()
    for load in loads:
        load.wait()

    def one_seed(s, carry):
        in_ref[s] = table[seed_ref[s]]
        rows = []
        for j in range(k2):
            row = table[hop1_ref[s * k2 + j]]
            in_ref[seeds + s * k2 + j] = row
            rows.append(row.astype(F32))
        mean_ref[s] = (tree_sum(rows) / k2).astype(BF16)
        return carry

    lax.fori_loop(0, seeds, one_seed, 0)

    def one_node(n, carry):
        for u in range(2):
            m = n * 2 + u
            rows = [table[hop2_ref[m * k1 + j]].astype(F32) for j in range(k1)]
            mean_ref[seeds + m] = (tree_sum(rows) / k1).astype(BF16)
        return carry

    lax.fori_loop(0, hop1 // 2, one_node, 0)


def gather_tree(seed, hop1, hop2, hot, cold):
    tile = hot.shape[1:]
    nodes = seed.shape[0] + hop1.shape[0]
    table_rows = hot.shape[0] + cold.shape[0]
    row_bytes = tile[0] * tile[1] * 2
    out = jax.ShapeDtypeStruct((nodes,) + tile, BF16)
    return pl.pallas_call(
        tree_kernel,
        out_shape=(out, out),
        in_specs=[pl.BlockSpec(memory_space=pltpu.SMEM)] * 3 + [pl.BlockSpec(memory_space=pl.ANY)] * 2,
        out_specs=(pl.BlockSpec(memory_space=pltpu.VMEM),) * 2,
        scratch_shapes=[
            pltpu.VMEM((table_rows,) + tile, BF16),
            pltpu.SemaphoreType.DMA((2,)),
        ],
        compiler_params=pltpu.CompilerParams(
            vmem_limit_bytes=(table_rows + 2 * nodes) * row_bytes + (8 << 20)
        ),
        cost_estimate=pl.CostEstimate(
            flops=0, bytes_accessed=8 * table_rows * row_bytes, transcendentals=0
        ),
        name="gather_tree",
    )(seed, hop1, hop2, hot, cold)


def reduce_kernel(
    mine0, mine1, away0, away1, out0, out1,
    got1, send2, got2, keep, send3, got3, send4, got4,
    s1, r1, s2, r2, s3, r3, s4, r4,
):
    mine, away, out = (mine0, mine1), (away0, away1), (out0, out1)
    hosts, planes = mine0.shape[0], mine0.shape[1]
    c, d, h = lax.axis_index("clique"), lax.axis_index("dp"), lax.axis_index("hst")
    host = [lax.rem(h + k, hosts) for k in range(hosts)]
    plane = [lax.rem(d + k, planes) for k in range(planes)]
    peers = [{"clique": 1 - c}] + [{"hst": q} for q in host[1:]] + [{"dp": p} for p in plane[1:]]

    barrier = pltpu.get_barrier_semaphore()
    for peer in peers:
        pl.semaphore_signal(barrier, inc=1, device_id=peer, device_id_type=pl.DeviceIdType.MESH)
    pl.semaphore_wait(barrier, len(peers))

    def send(src, dst, sent, landed, peer):
        copy = pltpu.make_async_remote_copy(
            src_ref=src, dst_ref=dst, send_sem=sent, recv_sem=landed,
            device_id=peer, device_id_type=pl.DeviceIdType.MESH,
        )
        copy.start()
        return copy

    first, second, third, fourth = {}, {}, {}, {}
    for m in range(2):
        for k in list(range(1, hosts)) + [0]:
            q = host[k]
            first[m, k] = send(
                away[m].at[q], got1.at[m, q], s1.at[m, k], r1.at[m, k], {"clique": 1 - c}
            )
    for m in range(2):
        for k in range(1, hosts):
            q = host[k]
            first[m, k].wait_recv()
            for p in range(planes):
                send2[m, k - 1, p] = (mine[m][q, p] + got1[m, q, p].astype(F32)).astype(BF16)
            second[m, k] = send(
                send2.at[m, k - 1], got2.at[m, k - 1], s2.at[m, k - 1], r2.at[m, k - 1], {"hst": q}
            )
        first[m, 0].wait_recv()
    for m in range(2):
        for k in range(1, hosts):
            second[m, k].wait_recv()
        for p in range(planes):
            total = mine[m][h, p] + got1[m, h, p].astype(F32)
            for k in range(1, hosts):
                total = total + got2[m, k - 1, p].astype(F32)
            keep[m, p] = total
            send3[m, p] = total.astype(BF16)
        for k in range(1, planes):
            third[m, k] = send(
                send3.at[m, plane[k]], got3.at[m, k - 1], s3.at[m, k - 1], r3.at[m, k - 1],
                {"dp": plane[k]},
            )
    for m in range(2):
        for k in range(1, planes):
            third[m, k].wait_recv()
        total = keep[m, d]
        for k in range(1, planes):
            total = total + got3[m, k - 1].astype(F32)
        send4[m] = total.astype(BF16)
        for k in range(1, planes):
            fourth[m, k] = send(
                send4.at[m], got4.at[m, k - 1], s4.at[m, k - 1], r4.at[m, k - 1], {"dp": plane[k]}
            )
        out[m][d] = send4[m].astype(F32)
    for m in range(2):
        for k in range(1, planes):
            fourth[m, k].wait_recv()
            out[m][lax.rem(d + planes - k, planes)] = got4[m, k - 1].astype(F32)
    for copies in (first, second, third, fourth):
        for copy in copies.values():
            copy.wait_send()


def reduce_pair(mine, away):
    hosts, planes, rows, width = mine[0].shape
    out = jax.ShapeDtypeStruct((planes, rows, width), F32)
    piece = (rows, width)
    return pl.pallas_call(
        reduce_kernel,
        out_shape=(out, out),
        in_specs=[pl.BlockSpec(memory_space=pltpu.VMEM)] * 4,
        out_specs=(pl.BlockSpec(memory_space=pltpu.VMEM),) * 2,
        scratch_shapes=[
            pltpu.VMEM((2, hosts, planes) + piece, BF16),
            pltpu.VMEM((2, hosts - 1, planes) + piece, BF16),
            pltpu.VMEM((2, hosts - 1, planes) + piece, BF16),
            pltpu.VMEM((2, planes) + piece, F32),
            pltpu.VMEM((2, planes) + piece, BF16),
            pltpu.VMEM((2, planes - 1) + piece, BF16),
            pltpu.VMEM((2,) + piece, BF16),
            pltpu.VMEM((2, planes - 1) + piece, BF16),
            pltpu.SemaphoreType.DMA((2, hosts)),
            pltpu.SemaphoreType.DMA((2, hosts)),
        ] + [pltpu.SemaphoreType.DMA((2, hosts - 1))] * 2 + [pltpu.SemaphoreType.DMA((2, planes - 1))] * 4,
        compiler_params=pltpu.CompilerParams(
            collective_id=0, has_side_effects=True, vmem_limit_bytes=40 << 20
        ),
        cost_estimate=pl.CostEstimate(flops=0, bytes_accessed=100 << 20, transcendentals=0),
        name="reduce_pair",
    )(*mine, *away)


def body(
    hot_table,
    cold_table,
    seed_source,
    hop1_source,
    hop2_source,
    cold_ask,
    cotangent,
    w1_self,
    w1_neigh,
    w2_self,
    w2_neigh,
):
    width = hot_table.shape[1]
    hidden_width = w1_self.shape[1]
    seeds = seed_source.shape[1]
    hop1 = hop1_source.shape[1]
    k2 = hop1 // seeds
    owners, cap = cold_ask.shape[1], cold_ask.shape[2]
    cliques = lax.axis_size("clique")
    hosts = lax.axis_size("hst")
    planes = lax.axis_size("dp")
    tile = (width // LANES, LANES)

    asked = lax.all_to_all(cold_ask[0], "hst", split_axis=0, concat_axis=0, tiled=True)
    hot_full = lax.all_gather(hot_table, "clique", axis=0, tiled=True)
    hot_full = hot_full.reshape((hot_full.shape[0],) + tile)
    cold_tiles = cold_table.reshape((cold_table.shape[0],) + tile)
    picked = pick_rows(asked.reshape(-1), cold_tiles).reshape((owners, cap) + tile)
    cold_rows = lax.all_to_all(picked, "hst", split_axis=0, concat_axis=0, tiled=True)
    cot_all = lax.all_gather(cotangent, ("clique", "dp", "hst"), axis=0, tiled=True)

    grad_seed = inner_cols(cotangent, w2_self)
    grad_mean = inner_cols(cotangent, w2_neigh) / k2

    in_tiles, mean_tiles = gather_tree(
        seed_source[0], hop1_source[0], hop2_source[0], hot_full, cold_rows.reshape((-1,) + tile)
    )
    level_in = in_tiles.reshape(-1, width)
    level_mean = mean_tiles.reshape(-1, width)

    pre = matmul(level_in, w1_self) + matmul(level_mean, w1_neigh)
    hidden = jnp.maximum(pre, 0.0).astype(BF16)
    hidden_seed = hidden[:seeds]
    node = lax.broadcasted_iota(jnp.int32, (seeds, hop1), 1) // k2
    member = (node == lax.broadcasted_iota(jnp.int32, (seeds, hop1), 0)).astype(BF16)
    hidden_mean = (matmul(member, hidden[seeds:]) / k2).astype(BF16)
    embedding = (matmul(hidden_seed, w2_self) + matmul(hidden_mean, w2_neigh)).astype(BF16)

    grad_hop = jnp.broadcast_to(grad_mean[:, None, :], (seeds, k2, hidden_width)).reshape(
        seeds * k2, hidden_width
    )
    grad_hidden = jnp.concatenate([grad_seed, grad_hop], 0)
    grad_pre = jnp.where(pre > 0, grad_hidden, 0.0).astype(BF16)

    shares2 = cliques * hosts
    both = jnp.stack([hidden_seed, hidden_mean], 1).reshape(seeds, 2, shares2, -1)
    both = lax.all_to_all(
        both.transpose(2, 0, 1, 3).reshape(shares2, seeds, -1),
        ("clique", "hst"), split_axis=0, concat_axis=0, tiled=True,
    )
    both = lax.all_gather(both.reshape(cliques, hosts * seeds, -1), "dp", axis=1)
    grad_w2 = inner_rows(both.reshape(cot_all.shape[0], -1), cot_all)

    me = lax.axis_index("clique")
    half = width // cliques
    rows = half // hosts // planes

    def terms(c):
        return [
            inner_rows(lax.dynamic_slice_in_dim(level, c * half, half, 1), grad_pre).reshape(
                hosts, planes, rows, hidden_width
            )
            for level in (level_in, level_mean)
        ]

    away = [t.astype(BF16) for t in terms(1 - me)]
    grad_w1 = [t.reshape(-1, hidden_width) for t in reduce_pair(terms(me), away)]

    cut = grad_w2.shape[0] // 2
    return (embedding, grad_w1[0], grad_w1[1], grad_w2[:cut], grad_w2[cut:])


def solution(mesh):
    workers = P(("clique", "dp", "hst"), None)
    rows = P(("clique", "hst"), None)
    in_specs = (
        P("clique", None), P("hst", None), workers, workers, workers,
        P(("clique", "dp", "hst"), None, None), workers, P(), P(), P(), P(),
    )
    return jax.shard_map(
        body, mesh=mesh, in_specs=in_specs, out_specs=(workers, rows, rows, rows, rows), check_vma=False
    )
```
